32 devices in a mesh: row: 8 (over y, x, core), col: 4 (over z).
Axes of the slice: x: 2, y: 2, z: 4, core: 2. Of those that a mesh axis runs over, the one named last changes fastest.
Arguments:
- values: float32 [4096, 4096], P('row', 'col'), may hold values from 0 to 10, as said below
- pattern: int32 [32, 32], replicated, may hold values from 0 to 1, as said below
- pruning: int32 [32, 32], replicated, may hold values from 0 to 1, as said below
- owners: int32 [32], replicated, may hold values from 0 to 31, as said below
Outputs:
- expanded: float32 [4096, 4096], P('row', 'col')
The draws below stay inside these ranges and needn't reach their ends.
Inputs may be any that keep to these rules, and one draw needn't show every extreme that they name: `values`: positive scores. `pattern`: every diagonal block is present. `pruning`: every diagonal block is kept. `owners`: A permutation of the 32 column blocks. Of the 8 column blocks of one index of col, at most 2 are stored at the column blocks of any one index of col, and exactly 2 at those of some index.
All inputs are finite; a program needn't handle non-finite values.
Results may differ from the reference program's by a relative error of at most 0.00065.
Values may be sent and summed in bfloat16 or wider, within the bound.
A program may use at most 128 MiB of HBM per device.

```python
import math
import jax
import jax.numpy as jnp
from jax import lax

NBLK = 32
NODES = 4096
CBD = 8
CAP = 2


def draw_values(key, part):
    key_base = jax.random.fold_in(key, 0)
    rows_pos = jnp.arange(NODES, dtype=jnp.float32)
    ramp = 1.0 + 2.0 * rows_pos / (NODES - 1)
    base = jnp.exp(jax.random.uniform(key_base, (NODES, NODES), jnp.float32, math.log(0.05), 0.0))
    return base * ramp[:, None]


def block_bits(key):
    bits = jax.random.randint(key, (NBLK, NBLK), 0, 2)
    diagonal = jnp.arange(NBLK)[:, None] == jnp.arange(NBLK)[None, :]
    return jnp.where(diagonal, 1, bits).astype(jnp.int32)


def draw_pattern(key, part):
    return block_bits(jax.random.fold_in(key, 11))


def draw_pruning(key, part):
    return block_bits(jax.random.fold_in(key, 23))


def draw_owners(key, part):
    ncols = NBLK // CBD
    key_order, key_turn, key_slot = jax.random.split(jax.random.fold_in(key, 37), 3)
    items = ncols * CAP
    scores = jax.random.permutation(key_order, items).astype(jnp.int32)
    item_ids = jnp.arange(items, dtype=jnp.int32)
    scores = jnp.where(item_ids < CAP, item_ids - CAP, scores)
    ordered = jnp.argsort(scores)
    residue = (ordered[:CBD] // CAP).astype(jnp.int32)
    turn = jax.random.randint(key_turn, (), 0, ncols).astype(jnp.int32)
    shifts = (residue + turn) % ncols
    slots = jax.random.permutation(key_slot, CBD).astype(jnp.int32)
    source = jnp.arange(NBLK, dtype=jnp.int32) // CBD
    within = jnp.arange(NBLK, dtype=jnp.int32) % CBD
    return ((source + shifts[within]) % ncols * CBD + slots[within]).astype(jnp.int32)


def setup_inputs(seed: int = 0) -> dict:
    key_of = jax.random.split(jax.random.key(seed), 5)
    values = draw_values(jax.random.fold_in(key_of[4], 71), 0)
    pattern = draw_pattern(jax.random.fold_in(key_of[4], 71), 0)
    pruning = draw_pruning(jax.random.fold_in(key_of[4], 71), 0)
    owners = draw_owners(jax.random.fold_in(key_of[4], 71), 0)
    return {"values": values, "pattern": pattern, "pruning": pruning, "owners": owners}


def expand_mask(tile, mask, blk):
    rows_in, cols_in = tile.shape
    shaped = tile.reshape(rows_in // blk, blk, cols_in // blk, blk)
    return (shaped * mask.astype(tile.dtype)[:, None, :, None]).reshape(rows_in, cols_in)


def reference(values, pattern, pruning, owners):
    nodes = values.shape[0]
    nblocks = pattern.shape[0]
    blk = nodes // nblocks
    masked = expand_mask(values, pattern, blk)
    colsum_in = jnp.sum(masked, axis=0)
    stochastic = (masked / colsum_in[None, :]).astype(jnp.bfloat16)
    widened = stochastic.astype(jnp.float32)
    square = jnp.dot(widened, widened, precision=lax.Precision.HIGHEST, preferred_element_type=jnp.float32)
    inflated = expand_mask(square * square, pruning, blk)
    colsum_out = jnp.sum(inflated, axis=0)
    normalized = NODES * inflated / colsum_out[None, :]
    column_blocks = normalized.reshape(nodes, nblocks, blk)
    placed = jnp.zeros_like(column_blocks).at[:, owners].set(column_blocks)
    return placed.reshape(nodes, nodes)
```

```python
import functools

import jax
import jax.numpy as jnp
from jax import lax
from jax.experimental import pallas as pl
from jax.experimental.pallas import tpu as pltpu
from jax.sharding import PartitionSpec as P

BLK = 128


def expand_mask(tile, mask, blk):
    rows_in, cols_in = tile.shape
    shaped = tile.reshape(rows_in // blk, blk, cols_in // blk, blk)
    return (shaped * mask.astype(tile.dtype)[:, None, :, None]).reshape(rows_in, cols_in)


def ranks_of(destination):
    width = destination.shape[-1]
    earlier = jnp.arange(width)[:, None] < jnp.arange(width)[None, :]
    same_dest = destination[..., :, None] == destination[..., None, :]
    return jnp.sum(jnp.where(same_dest & earlier, 1, 0), axis=-2).astype(jnp.int32)


def pack_blocks(tile, owners, me_col, ncols, capacity, blk):
    rows_in, cols_in = tile.shape
    width = cols_in // blk
    my_owners = lax.dynamic_slice(owners, (me_col * width,), (width,))
    destination = my_owners // width
    rank = ranks_of(destination)
    slot_ids = jnp.arange(ncols * capacity)
    selector = (
        (destination[None, :] == (slot_ids // capacity)[:, None])
        & (rank[None, :] == (slot_ids % capacity)[:, None])
    ).astype(tile.dtype)
    column_blocks = tile.reshape(rows_in, width, blk)
    outgoing = jnp.einsum(
        "pk,rkb->prb",
        selector,
        column_blocks,
        preferred_element_type=jnp.float32,
        precision=lax.Precision.HIGHEST,
    )
    return outgoing.astype(tile.dtype)


def unpack_blocks(arrived, owners, me_col, ncols, capacity):
    slot_count, rows_in, blk = arrived.shape
    width = owners.shape[0] // ncols
    table = owners.reshape(ncols, width)
    rank = ranks_of(table // width)
    wanted = me_col * width + jnp.arange(width)
    matches = table[None, :, :] == wanted[:, None, None]
    which_slot = rank[:, :, None] == jnp.arange(capacity)[None, None, :]
    selector = jnp.sum(jnp.where(matches[:, :, :, None] & which_slot[None], 1, 0), axis=2)
    selector = selector.reshape(width, ncols * capacity).astype(arrived.dtype)
    placed = jnp.einsum(
        "sp,prb->rsb",
        selector,
        arrived,
        preferred_element_type=jnp.float32,
        precision=lax.Precision.HIGHEST,
    )
    return placed.reshape(rows_in, width * blk).astype(arrived.dtype)


def body(values, pattern, pruning, owners):
    rows_dev, cols_dev = values.shape
    blk = BLK
    row_blocks = rows_dev // blk
    col_blocks = cols_dev // blk
    ncols = lax.axis_size("col")
    capacity = max(2, (col_blocks + ncols - 1) // ncols)
    me_row = lax.axis_index("row")
    me_col = lax.axis_index("col")
    local_pattern = lax.dynamic_slice(
        pattern, (me_row * row_blocks, me_col * col_blocks), (row_blocks, col_blocks)
    )
    masked = expand_mask(values, local_pattern, blk)
    colsum_in = lax.psum(jnp.sum(masked, axis=0), "row")
    stochastic = (masked / colsum_in[None, :]).astype(jnp.bfloat16)
    row_panel = lax.all_gather(stochastic, "col", axis=1, tiled=True)
    nodes = row_panel.shape[1]
    pruning_rows = lax.dynamic_slice(
        pruning, (me_row * row_blocks, 0), (row_blocks, pruning.shape[1])
    )
    arrived = lax.all_to_all(
        pack_blocks(stochastic, owners, me_col, ncols, capacity, blk),
        "col",
        split_axis=0,
        concat_axis=0,
        tiled=True,
    )
    right_operand = unpack_blocks(arrived, owners, me_col, ncols, capacity)
    wanted = me_col * col_blocks + jnp.arange(col_blocks)
    relocate = (owners[:, None] == wanted[None, :]).astype(jnp.float32)
    kept_mask = jnp.dot(pruning_rows.astype(jnp.float32), relocate, precision=lax.Precision.HIGHEST)
    square = jnp.dot(
        row_panel,
        lax.all_gather(right_operand, "row", axis=0, tiled=True),
        preferred_element_type=jnp.float32,
    )
    inflated = expand_mask(square * square, kept_mask, blk)
    colsum_out = lax.psum(jnp.sum(inflated, axis=0), "row")
    normalized = jnp.float32(nodes) * inflated / colsum_out[None, :]
    return normalized


MESH = pl.DeviceIdType.MESH


def tables(pattern, pruning, owners, rows_b, cols_b, ncols):
    me_row = lax.axis_index("row")
    me_col = lax.axis_index("col")
    nblk = owners.shape[0]
    ids = jnp.arange(nblk)
    source = ids // cols_b
    dest = owners // cols_b
    same = (source[:, None] == source[None, :]) & (dest[:, None] == dest[None, :])
    rank = jnp.sum(jnp.where(same & (ids[:, None] < ids[None, :]), 1, 0), axis=0)
    cap = cols_b // ncols
    packed = source * cols_b + dest * cap + rank
    order = jnp.sum(jnp.where(packed[None, :] == ids[:, None], ids[None, :], 0), axis=1)
    wanted = me_col * cols_b + jnp.arange(cols_b)
    hit = owners[None, :] == wanted[:, None]
    pos = jnp.sum(jnp.where(hit, (source * cap + rank)[None, :], 0), axis=1)
    from_block = jnp.sum(jnp.where(hit, ids[None, :], 0), axis=1)
    mine = lax.dynamic_slice(order, (me_col * cols_b,), (cols_b,))
    prow = lax.dynamic_slice(pattern, (me_row * rows_b, 0), (rows_b, nblk))
    prow = jnp.sum(jnp.where(mine[None, :, None] == ids[None, None, :], prow[:, None, :], 0), axis=2)
    krow = lax.dynamic_slice(pruning, (me_row * rows_b, 0), (rows_b, nblk))
    kept = jnp.sum(jnp.where(from_block[None, :, None] == ids[None, None, :], krow[:, None, :], 0), axis=2)
    return jnp.concatenate(
        [order, pos, prow.reshape(-1), kept.reshape(-1), mine - me_col * cols_b]
    ).astype(jnp.int32)


def kernel(n, nodes, tab, values, out, tiles, right, scores, work, sums_a, sums_b, rhs,
           load_sem, zs, zr, xs, xr, as_, ar, bs, br):
    rows, cols = values.shape
    blk = BLK
    rows_b, cols_b = rows // blk, cols // blk
    nblk = n * cols_b
    wide = cols // n
    each = cols_b // n
    half = rows_b // 2
    loads = [
        pltpu.make_async_copy(values.at[:, pl.ds(b * blk, blk)], scores.at[b], load_sem.at[b])
        for b in range(cols_b)
    ]
    for load in loads:
        load.start()
    r = lax.axis_index("row")
    c = lax.axis_index("col")
    core, px, py = r % 2, (r // 2) % 2, r // 4

    def at(fy, fx, fc):
        y = 1 - py if fy else py
        x = 1 - px if fx else px
        k = 1 - core if fc else core
        return y * 4 + x * 2 + k

    others = [at(f // 4, (f // 2) % 2, f % 2) for f in range(1, 8)]

    barrier = pltpu.get_barrier_semaphore()
    for peer in others:
        pl.semaphore_signal(barrier, inc=1, device_id={"row": peer}, device_id_type=MESH)

    @pl.when(c > 0)
    def _():
        pl.semaphore_signal(barrier, inc=1, device_id={"col": c - 1}, device_id_type=MESH)

    @pl.when(c < n - 1)
    def _():
        pl.semaphore_signal(barrier, inc=1, device_id={"col": c + 1}, device_id_type=MESH)

    def total_over_row(sums, ssem, rsem):
        for f, peer in enumerate(others):
            pltpu.make_async_remote_copy(
                src_ref=sums.at[0], dst_ref=sums.at[f + 1], send_sem=ssem.at[f], recv_sem=rsem.at[f],
                device_id={"row": peer}, device_id_type=MESH).start()
        for f, peer in enumerate(others):
            pltpu.make_async_remote_copy(
                src_ref=sums.at[0], dst_ref=sums.at[f + 1], send_sem=ssem.at[f], recv_sem=rsem.at[f],
                device_id={"row": peer}, device_id_type=MESH).wait()
        terms = [sums[f] for f in range(8)]
        pair = [terms[i] + terms[i + 1] for i in range(0, 8, 2)]
        quad = [pair[0] + pair[1], pair[2] + pair[3]]
        return quad[0] + quad[1]

    for load in loads:
        load.wait()
    masks = nblk + cols_b
    local = masks + 2 * rows_b * cols_b
    for p in range(cols_b):
        b = tab[local + p]
        acc = jnp.zeros((1, blk), jnp.float32)
        for i in range(rows_b):
            keep = tab[masks + i * cols_b + p].astype(jnp.float32)
            x = scores[b, pl.ds(i * blk, blk), :] * keep
            work[p, pl.ds(i * blk, blk), :] = x
            acc = acc + jnp.sum(x, axis=0, keepdims=True)
        sums_a[0, :, pl.ds(p * blk, blk)] = acc

    ends = jnp.where(c == 0, 1, 0) + jnp.where(c == n - 1, 1, 0)
    pl.semaphore_wait(barrier, 9 - ends)

    colsum = total_over_row(sums_a, as_, ar)
    for p in range(cols_b):
        part = work[p] / colsum[:, p * blk:(p + 1) * blk]
        tiles[c, p // each, :, pl.ds(p % each * blk, blk)] = part.astype(jnp.bfloat16)

    def zcopy(way, d, q, source):
        target = c - 1 if way == 0 else c + 1
        return pltpu.make_async_remote_copy(
            src_ref=tiles.at[source, q], dst_ref=tiles.at[source, q],
            send_sem=zs.at[way, d, q], recv_sem=zr.at[way, d, q],
            device_id={"col": target}, device_id_type=MESH)

    def zarrive(way, d, q, source):
        peer = c + 1 if way == 0 else c - 1
        pltpu.make_async_remote_copy(
            src_ref=tiles.at[source, q], dst_ref=tiles.at[source, q],
            send_sem=zs.at[way, d, q], recv_sem=zr.at[way, d, q],
            device_id={"col": peer}, device_id_type=MESH).wait_recv()

    side_x, side_y, side_c = at(0, 1, 0), at(1, 0, 0), at(0, 0, 1)
    diag = at(1, 1, 0)

    def region(u, who, part):
        if part is None:
            return right.at[u, pl.ds(who * rows_b, rows_b)]
        return right.at[u, pl.ds(who * rows_b + part * half, half)]

    def sent(u, k):
        src, dst, to = [
            (region(u, r, None), region(u, r, None), side_x),
            (region(u, r, None), region(u, r, None), side_y),
            (region(u, r, None), region(u, r, None), side_c),
            (region(u, side_x, 0), region(u, side_x, 0), side_y),
            (region(u, side_y, 1), region(u, side_y, 1), side_x),
            (region(u, side_x, None), region(u, side_x, None), side_c),
            (region(u, side_y, None), region(u, side_y, None), side_c),
            (region(u, diag, 0), region(u, diag, 0), side_c),
            (region(u, diag, 1), region(u, diag, 1), side_c),
        ][k]
        return pltpu.make_async_remote_copy(
            src_ref=src, dst_ref=dst, send_sem=xs.at[u, k], recv_sem=xr.at[u, k],
            device_id={"row": to}, device_id_type=MESH)

    def landed(u, k):
        where, to = [
            (region(u, side_x, None), side_x),
            (region(u, side_y, None), side_y),
            (region(u, side_c, None), side_c),
            (region(u, diag, 0), side_y),
            (region(u, diag, 1), side_x),
            (region(u, at(0, 1, 1), None), side_c),
            (region(u, at(1, 0, 1), None), side_c),
            (region(u, at(1, 1, 1), 0), side_c),
            (region(u, at(1, 1, 1), 1), side_c),
        ][k]
        pltpu.make_async_remote_copy(
            src_ref=where, dst_ref=where, send_sem=xs.at[u, k], recv_sem=xr.at[u, k],
            device_id={"row": to}, device_id_type=MESH).wait_recv()

    def begin(u):
        right[u, pl.ds(r * rows_b, rows_b)] = tiles[u, c].reshape(rows_b, blk, wide)
        for k in range(3):
            sent(u, k).start()

    def second(u):
        landed(u, 0)
        sent(u, 3).start()
        sent(u, 5).start()
        landed(u, 1)
        sent(u, 4).start()
        sent(u, 6).start()

    def third(u):
        landed(u, 3)
        sent(u, 7).start()
        landed(u, 4)
        sent(u, 8).start()

    for i in range(n):
        @pl.when(c > 0)
        def _():
            zcopy(0, 0, i, c).start()

        @pl.when(c < n - 1)
        def _():
            zcopy(1, 0, n - 1 - i, c).start()
        if i == 0:
            begin(c)

    def begun_at(stage, act):
        if stage == -1:
            act(c)
        for d in range(1, n):
            @pl.when((c == stage) & (c + d < n))
            def _():
                act(c + d)

            @pl.when((n - 1 - c == stage) & (c - d >= 0))
            def _():
                act(c - d)

    for i in range(n + 1):
        if i < n:
            for d in range(1, n):
                @pl.when(c + d < n)
                def _():
                    zarrive(0, d - 1, i, c + d)

                    @pl.when(c > 0)
                    def _():
                        if d < n - 1:
                            zcopy(0, d, i, c + d).start()

                    @pl.when(c == i)
                    def _():
                        begin(c + d)

                @pl.when(c - d >= 0)
                def _():
                    zarrive(1, d - 1, n - 1 - i, c - d)

                    @pl.when(c < n - 1)
                    def _():
                        if d < n - 1:
                            zcopy(1, d, n - 1 - i, c - d).start()

                    @pl.when(c == n - 1 - i)
                    def _():
                        begin(c - d)
        begun_at(i - 1, second)
        begun_at(i - 2, third)
    begun_at(n - 1, third)

    for u in range(n):
        for k in (2, 5, 6, 7, 8):
            landed(u, k)

    for z in range(n):
        def product(u, carry):
            for p in range(cols_b):
                rhs[pl.ds(p * blk, blk), :] = right[u, tab[z * cols_b + p]]
            lhs = jnp.concatenate([tiles[z, q] for q in range(n)], axis=1)
            part = jnp.dot(lhs, rhs[...], preferred_element_type=jnp.float32)
            for k in range(each):
                cut = part[:, k * blk:(k + 1) * blk]
                if z == 0:
                    work[u * each + k] = cut
                else:
                    work[u * each + k] += cut
            return carry
        lax.fori_loop(0, n, product, 0)

    for s in range(cols_b):
        p = tab[nblk + s]
        acc = jnp.zeros((1, blk), jnp.float32)
        for i in range(rows_b):
            keep = tab[masks + rows_b * cols_b + i * cols_b + s].astype(jnp.float32)
            x = work[p, pl.ds(i * blk, blk), :]
            x = x * x * keep
            out[pl.ds(i * blk, blk), pl.ds(s * blk, blk)] = x
            acc = acc + jnp.sum(x, axis=0, keepdims=True)
        sums_b[0, :, pl.ds(s * blk, blk)] = acc
    colsum = total_over_row(sums_b, bs, br)
    out[...] = (jnp.float32(nodes) * out[...]) / colsum

    for i in range(n):
        for d in range(n - 1):
            @pl.when((c > 0) & (c + d < n))
            def _():
                zcopy(0, d, i, c + d).wait_send()

            @pl.when((c < n - 1) & (c - d >= 0))
            def _():
                zcopy(1, d, i, c - d).wait_send()
    for u in range(n):
        for k in range(9):
            sent(u, k).wait_send()


def fused(values, pattern, pruning, owners):
    rows, cols = values.shape
    n = lax.axis_size("col")
    nodes = n * cols
    tab = tables(pattern, pruning, owners, rows // BLK, cols // BLK, n)
    dma = pltpu.SemaphoreType.DMA
    return pl.pallas_call(
        functools.partial(kernel, n, nodes),
        out_shape=jax.ShapeDtypeStruct((rows, cols), jnp.float32),
        in_specs=[pl.BlockSpec(memory_space=pltpu.SMEM), pl.BlockSpec(memory_space=pl.ANY)],
        out_specs=pl.BlockSpec(memory_space=pltpu.VMEM),
        scratch_shapes=[
            pltpu.VMEM((n, n, rows, cols // n), jnp.bfloat16),
            pltpu.VMEM((n, nodes // BLK, BLK, cols // n), jnp.bfloat16),
            pltpu.VMEM((cols // BLK, rows, BLK), jnp.float32),
            pltpu.VMEM((cols // BLK, rows, BLK), jnp.float32),
            pltpu.VMEM((8, 1, cols), jnp.float32),
            pltpu.VMEM((8, 1, cols), jnp.float32),
            pltpu.VMEM((cols, cols // n), jnp.bfloat16),
            dma((cols // BLK,)),
            dma((2, n - 1, n)),
            dma((2, n - 1, n)),
            dma((n, 9)),
            dma((n, 9)),
            dma((7,)),
            dma((7,)),
            dma((7,)),
            dma((7,)),
        ],
        compiler_params=pltpu.CompilerParams(
            collective_id=0, has_side_effects=True, vmem_limit_bytes=44 * 2**20
        ),
        cost_estimate=pl.CostEstimate(
            flops=2 * rows * nodes * cols, bytes_accessed=8 * rows * cols, transcendentals=0
        ),
    )(tab, values)


def solution(mesh):
    nrows, ncols = mesh.shape["row"], mesh.shape["col"]

    def program(values, pattern, pruning, owners):
        rows, cols = values.shape
        packed = nrows == 8 and owners.shape[0] == 2 * ncols * ncols
        return (fused if packed else body)(values, pattern, pruning, owners)

    return jax.shard_map(
        program,
        mesh=mesh,
        in_specs=(P("row", "col"), P(), P(), P()),
        out_specs=P("row", "col"),
        check_vma=False,
    )
```

```python
import functools

import jax
import jax.numpy as jnp
from jax import lax
from jax.experimental import pallas as pl
from jax.experimental.pallas import tpu as pltpu
from jax.sharding import PartitionSpec as P

BLK = 128


def expand_mask(tile, mask, blk):
    rows_in, cols_in = tile.shape
    shaped = tile.reshape(rows_in // blk, blk, cols_in // blk, blk)
    return (shaped * mask.astype(tile.dtype)[:, None, :, None]).reshape(rows_in, cols_in)


def ranks_of(destination):
    width = destination.shape[-1]
    earlier = jnp.arange(width)[:, None] < jnp.arange(width)[None, :]
    same_dest = destination[..., :, None] == destination[..., None, :]
    return jnp.sum(jnp.where(same_dest & earlier, 1, 0), axis=-2).astype(jnp.int32)


def pack_blocks(tile, owners, me_col, ncols, capacity, blk):
    rows_in, cols_in = tile.shape
    width = cols_in // blk
    my_owners = lax.dynamic_slice(owners, (me_col * width,), (width,))
    destination = my_owners // width
    rank = ranks_of(destination)
    slot_ids = jnp.arange(ncols * capacity)
    selector = (
        (destination[None, :] == (slot_ids // capacity)[:, None])
        & (rank[None, :] == (slot_ids % capacity)[:, None])
    ).astype(tile.dtype)
    column_blocks = tile.reshape(rows_in, width, blk)
    outgoing = jnp.einsum(
        "pk,rkb->prb",
        selector,
        column_blocks,
        preferred_element_type=jnp.float32,
        precision=lax.Precision.HIGHEST,
    )
    return outgoing.astype(tile.dtype)


def unpack_blocks(arrived, owners, me_col, ncols, capacity):
    slot_count, rows_in, blk = arrived.shape
    width = owners.shape[0] // ncols
    table = owners.reshape(ncols, width)
    rank = ranks_of(table // width)
    wanted = me_col * width + jnp.arange(width)
    matches = table[None, :, :] == wanted[:, None, None]
    which_slot = rank[:, :, None] == jnp.arange(capacity)[None, None, :]
    selector = jnp.sum(jnp.where(matches[:, :, :, None] & which_slot[None], 1, 0), axis=2)
    selector = selector.reshape(width, ncols * capacity).astype(arrived.dtype)
    placed = jnp.einsum(
        "sp,prb->rsb",
        selector,
        arrived,
        preferred_element_type=jnp.float32,
        precision=lax.Precision.HIGHEST,
    )
    return placed.reshape(rows_in, width * blk).astype(arrived.dtype)


def body(values, pattern, pruning, owners):
    rows_dev, cols_dev = values.shape
    blk = BLK
    row_blocks = rows_dev // blk
    col_blocks = cols_dev // blk
    ncols = lax.axis_size("col")
    capacity = max(2, (col_blocks + ncols - 1) // ncols)
    me_row = lax.axis_index("row")
    me_col = lax.axis_index("col")
    local_pattern = lax.dynamic_slice(
        pattern, (me_row * row_blocks, me_col * col_blocks), (row_blocks, col_blocks)
    )
    masked = expand_mask(values, local_pattern, blk)
    colsum_in = lax.psum(jnp.sum(masked, axis=0), "row")
    stochastic = (masked / colsum_in[None, :]).astype(jnp.bfloat16)
    row_panel = lax.all_gather(stochastic, "col", axis=1, tiled=True)
    nodes = row_panel.shape[1]
    pruning_rows = lax.dynamic_slice(
        pruning, (me_row * row_blocks, 0), (row_blocks, pruning.shape[1])
    )
    arrived = lax.all_to_all(
        pack_blocks(stochastic, owners, me_col, ncols, capacity, blk),
        "col",
        split_axis=0,
        concat_axis=0,
        tiled=True,
    )
    right_operand = unpack_blocks(arrived, owners, me_col, ncols, capacity)
    wanted = me_col * col_blocks + jnp.arange(col_blocks)
    relocate = (owners[:, None] == wanted[None, :]).astype(jnp.float32)
    kept_mask = jnp.dot(pruning_rows.astype(jnp.float32), relocate, precision=lax.Precision.HIGHEST)
    square = jnp.dot(
        row_panel,
        lax.all_gather(right_operand, "row", axis=0, tiled=True),
        preferred_element_type=jnp.float32,
    )
    inflated = expand_mask(square * square, kept_mask, blk)
    colsum_out = lax.psum(jnp.sum(inflated, axis=0), "row")
    normalized = jnp.float32(nodes) * inflated / colsum_out[None, :]
    return normalized


MESH = pl.DeviceIdType.MESH


def kernel(n, nodes, own, pattern, pruning, values, out, tiles, right, scores, work, left, late,
           sums_a, sums_b, invs, rhs, tab, load_sem, zs, zr, xs, xr, as_, ar, bs, br, cs, cr):
    rows, cols = values.shape
    blk = BLK
    rows_b, cols_b = rows // blk, cols // blk
    nblk = n * cols_b
    wide = cols // n
    each = cols_b // n
    half = rows_b // 2
    loads = [
        pltpu.make_async_copy(values.at[:, pl.ds(b * blk, blk)], scores.at[b], load_sem.at[b])
        for b in range(cols_b)
    ]
    for load in loads:
        load.start()
    r = lax.axis_index("row")
    c = lax.axis_index("col")
    core, px, py = r % 2, (r // 2) % 2, r // 4

    def at(fy, fx, fc):
        y = 1 - py if fy else py
        x = 1 - px if fx else px
        k = 1 - core if fc else core
        return y * 4 + x * 2 + k

    others = [at(f // 4, (f // 2) % 2, f % 2) for f in range(1, 8)]

    barrier = pltpu.get_barrier_semaphore()
    for peer in others:
        pl.semaphore_signal(barrier, inc=1, device_id={"row": peer}, device_id_type=MESH)
    for d in range(1, n):
        pl.semaphore_signal(barrier, inc=1, device_id={"col": (c + d) % n}, device_id_type=MESH)

    def chosen(keys, key, options):
        found = options[0]
        for k, option in zip(keys[1:], options[1:]):
            found = jnp.where(k == key, option, found)
        return found

    def order_of(base):
        dest = [lax.div(own[base + k], cols_b) for k in range(cols_b)]
        place = []
        for k in range(cols_b):
            rank = sum([jnp.where(dest[i] == dest[k], 1, 0) for i in range(k)], 0)
            place.append(dest[k] * each + rank)
        return [chosen(place, p, range(cols_b)) for p in range(cols_b)]

    def row_copies(sums, ssem, rsem):
        return [
            pltpu.make_async_remote_copy(
                src_ref=sums.at[0], dst_ref=sums.at[f + 1], send_sem=ssem.at[f], recv_sem=rsem.at[f],
                device_id={"row": peer}, device_id_type=MESH)
            for f, peer in enumerate(others)
        ]

    def total_of(sums):
        terms = [sums[f] for f in range(8)]
        pair = [terms[i] + terms[i + 1] for i in range(0, 8, 2)]
        return (pair[0] + pair[1]) + (pair[2] + pair[3])

    def zcopy(way, d, q, source):
        target = c - 1 if way == 0 else c + 1
        return pltpu.make_async_remote_copy(
            src_ref=tiles.at[source, q], dst_ref=tiles.at[source, q],
            send_sem=zs.at[way, d, q], recv_sem=zr.at[way, d, q],
            device_id={"col": target}, device_id_type=MESH)

    def zarrive(way, d, q, source):
        peer = c + 1 if way == 0 else c - 1
        pltpu.make_async_remote_copy(
            src_ref=tiles.at[source, q], dst_ref=tiles.at[source, q],
            send_sem=zs.at[way, d, q], recv_sem=zr.at[way, d, q],
            device_id={"col": peer}, device_id_type=MESH).wait_recv()

    side_x, side_y, side_c = at(0, 1, 0), at(1, 0, 0), at(0, 0, 1)
    diag = at(1, 1, 0)

    def region(u, who, part):
        if part is None:
            return right.at[u, pl.ds(who * rows_b, rows_b)]
        return right.at[u, pl.ds(who * rows_b + part * half, half)]

    def sent(u, k):
        src, dst, to = [
            (region(u, r, None), region(u, r, None), side_x),
            (region(u, r, None), region(u, r, None), side_y),
            (region(u, r, None), region(u, r, None), side_c),
            (region(u, side_x, 0), region(u, side_x, 0), side_y),
            (region(u, side_y, 1), region(u, side_y, 1), side_x),
            (region(u, side_x, None), region(u, side_x, None), side_c),
            (region(u, side_y, None), region(u, side_y, None), side_c),
            (region(u, diag, 0), region(u, diag, 0), side_c),
            (region(u, diag, 1), region(u, diag, 1), side_c),
        ][k]
        return pltpu.make_async_remote_copy(
            src_ref=src, dst_ref=dst, send_sem=xs.at[u, k], recv_sem=xr.at[u, k],
            device_id={"row": to}, device_id_type=MESH)

    def landed(u, k):
        where, to = [
            (region(u, side_x, None), side_x),
            (region(u, side_y, None), side_y),
            (region(u, side_c, None), side_c),
            (region(u, diag, 0), side_y),
            (region(u, diag, 1), side_x),
            (region(u, at(0, 1, 1), None), side_c),
            (region(u, at(1, 0, 1), None), side_c),
            (region(u, at(1, 1, 1), 0), side_c),
            (region(u, at(1, 1, 1), 1), side_c),
        ][k]
        pltpu.make_async_remote_copy(
            src_ref=where, dst_ref=where, send_sem=xs.at[u, k], recv_sem=xr.at[u, k],
            device_id={"row": to}, device_id_type=MESH).wait_recv()

    def begin(u):
        right[u, pl.ds(r * rows_b, rows_b)] = tiles[u, c].reshape(rows_b, blk, wide)
        for k in range(3):
            sent(u, k).start()

    def second(u):
        landed(u, 0)
        sent(u, 3).start()
        sent(u, 5).start()
        landed(u, 1)
        sent(u, 4).start()
        sent(u, 6).start()

    def third(u):
        landed(u, 3)
        sent(u, 7).start()
        landed(u, 4)
        sent(u, 8).start()

    mine = order_of(c * cols_b)
    for load in loads:
        load.wait()
    pl.semaphore_wait(barrier, 7 + n - 1)
    made = []
    for i in range((n + 1) // 2):
        made += [i, n - 1 - i] if i != n - 1 - i else [i]
    for q in made:
        for k in range(each):
            b = mine[q * each + k]
            acc = jnp.zeros((1, blk), jnp.float32)
            for i in range(rows_b):
                keep = pattern[r * rows_b + i, c * cols_b + b].astype(jnp.float32)
                x = scores[b, pl.ds(i * blk, blk), :] * keep
                tiles[c, q, pl.ds(i * blk, blk), pl.ds(k * blk, blk)] = x.astype(jnp.bfloat16)
                acc = acc + jnp.sum(x, axis=0, keepdims=True)
            sums_a[0, q, :, pl.ds(k * blk, blk)] = acc

        @pl.when(c > 0)
        def _():
            zcopy(0, 0, q, c).start()

        @pl.when(c < n - 1)
        def _():
            zcopy(1, 0, q, c).start()
    for copy in row_copies(sums_a, as_, ar):
        copy.start()
    begin(c)

    for z in range(n):
        for p, b in enumerate(order_of(z * cols_b)):
            tab[z * cols_b + p] = z * cols_b + b
    came = [tab[u * cols_b + c * each + k] for u in range(n) for k in range(each)]
    goes = [own[b] - c * cols_b for b in came]

    for copy in row_copies(sums_a, as_, ar):
        copy.wait()
    invs[c] = 1.0 / total_of(sums_a)

    def scales(d):
        return pltpu.make_async_remote_copy(
            src_ref=invs.at[c], dst_ref=invs.at[c], send_sem=cs.at[d - 1], recv_sem=cr.at[d - 1],
            device_id={"col": (c + d) % n}, device_id_type=MESH)

    for d in range(1, n):
        scales(d).start()

    def scales_landed():
        for d in range(1, n):
            source = (c + n - d) % n
            pltpu.make_async_remote_copy(
                src_ref=invs.at[source], dst_ref=invs.at[source],
                send_sem=cs.at[d - 1], recv_sem=cr.at[d - 1],
                device_id={"col": source}, device_id_type=MESH).wait_recv()

    last = jnp.where(c < n // 2, n - 1, 0)

    def scaled(z, q):
        return (tiles[z, q].astype(jnp.float32) * invs[z, q]).astype(jnp.bfloat16)

    def early_product():
        scales_landed()
        for u in range(n):
            for k in (2, 5, 6, 7, 8):
                landed(u, k)
        for z in range(n):
            for j in range(n - 1):
                left[:, pl.ds(j * wide, wide)] = scaled(z, (last + 1 + j) % n)

            def product(u, carry):
                for j in range(n - 1):
                    q = (last + 1 + j) % n
                    for k in range(each):
                        rhs[pl.ds((j * each + k) * blk, blk), :] = right[u, tab[z * cols_b + q * each + k]]
                part = jnp.dot(
                    left[...], rhs[pl.ds(0, (n - 1) * wide), :], preferred_element_type=jnp.float32)
                for k in range(each):
                    cut = part[:, k * blk:(k + 1) * blk]
                    if z == 0:
                        work[u * each + k] = cut
                    else:
                        work[u * each + k] += cut
                return carry
            lax.fori_loop(0, n, product, 0)

    def late_product():
        for z in range(n):
            late[:, pl.ds(z * wide, wide)] = scaled(z, last)

        def product(u, carry):
            for z in range(n):
                for k in range(each):
                    rhs[pl.ds((z * each + k) * blk, blk), :] = right[u, tab[z * cols_b + last * each + k]]
            part = jnp.dot(late[...], rhs[...], preferred_element_type=jnp.float32)
            scale = invs[u, c]
            for k in range(each):
                piece = slice(k * blk, (k + 1) * blk)
                work[u * each + k] = (work[u * each + k] + part[:, piece]) * scale[:, piece]
            return carry
        lax.fori_loop(0, n, product, 0)

    at_end = (c == 0) | (c == n - 1)

    def begun_at(stage, act):
        if stage == -1:
            act(c)
        for d in range(1, n):
            @pl.when((c == stage) & (c + d < n))
            def _():
                act(c + d)

            @pl.when((n - 1 - c == stage) & (c - d >= 0))
            def _():
                act(c - d)

    for i in range(n + 1):
        if i == n - 1:
            @pl.when(at_end)
            def _():
                early_product()
        if i < n:
            for d in range(1, n):
                @pl.when(c + d < n)
                def _():
                    zarrive(0, d - 1, i, c + d)

                    @pl.when(c > 0)
                    def _():
                        if d < n - 1:
                            zcopy(0, d, i, c + d).start()

                    @pl.when(c == i)
                    def _():
                        begin(c + d)

                @pl.when(c - d >= 0)
                def _():
                    zarrive(1, d - 1, n - 1 - i, c - d)

                    @pl.when(c < n - 1)
                    def _():
                        if d < n - 1:
                            zcopy(1, d, n - 1 - i, c - d).start()

                    @pl.when(c == n - 1 - i)
                    def _():
                        begin(c - d)
        begun_at(i - 1, second)
        begun_at(i - 2, third)
    begun_at(n - 1, third)

    @pl.when(jnp.logical_not(at_end))
    def _():
        early_product()

    late_product()

    for s in range(cols_b):
        p = chosen(goes, s, range(cols_b))
        b = chosen(goes, s, came)
        acc = jnp.zeros((1, blk), jnp.float32)
        for i in range(rows_b):
            keep = pruning[r * rows_b + i, b].astype(jnp.float32)
            x = work[p, pl.ds(i * blk, blk), :]
            x = x * x * keep
            out[pl.ds(i * blk, blk), pl.ds(s * blk, blk)] = x
            acc = acc + jnp.sum(x, axis=0, keepdims=True)
        sums_b[0, :, pl.ds(s * blk, blk)] = acc
    for copy in row_copies(sums_b, bs, br):
        copy.start()
    for copy in row_copies(sums_b, bs, br):
        copy.wait()
    inv_out = 1.0 / total_of(sums_b)
    out[...] = (out[...] * inv_out) * jnp.float32(nodes)

    for d in range(1, n):
        scales(d).wait_send()
    for i in range(n):
        for d in range(n - 1):
            @pl.when((c > 0) & (c + d < n))
            def _():
                zcopy(0, d, i, c + d).wait_send()

            @pl.when((c < n - 1) & (c - d >= 0))
            def _():
                zcopy(1, d, i, c - d).wait_send()
    for u in range(n):
        for k in range(9):
            sent(u, k).wait_send()


def fused(values, pattern, pruning, owners):
    rows, cols = values.shape
    n = lax.axis_size("col")
    nodes = n * cols
    dma = pltpu.SemaphoreType.DMA
    return pl.pallas_call(
        functools.partial(kernel, n, nodes),
        out_shape=jax.ShapeDtypeStruct((rows, cols), jnp.float32),
        in_specs=[pl.BlockSpec(memory_space=pltpu.SMEM)] * 3 + [pl.BlockSpec(memory_space=pl.ANY)],
        out_specs=pl.BlockSpec(memory_space=pltpu.VMEM),
        scratch_shapes=[
            pltpu.VMEM((n, n, rows, cols // n), jnp.bfloat16),
            pltpu.VMEM((n, nodes // BLK, BLK, cols // n), jnp.bfloat16),
            pltpu.VMEM((cols // BLK, rows, BLK), jnp.float32),
            pltpu.VMEM((cols // BLK, rows, BLK), jnp.float32),
            pltpu.VMEM((rows, cols - cols // n), jnp.bfloat16),
            pltpu.VMEM((rows, cols), jnp.bfloat16),
            pltpu.VMEM((8, n, 1, cols // n), jnp.float32),
            pltpu.VMEM((8, 1, cols), jnp.float32),
            pltpu.VMEM((n, n, 1, cols // n), jnp.float32),
            pltpu.VMEM((cols, cols // n), jnp.bfloat16),
            pltpu.SMEM((nodes // BLK,), jnp.int32),
            dma((cols // BLK,)),
            dma((2, n - 1, n)),
            dma((2, n - 1, n)),
            dma((n, 9)),
            dma((n, 9)),
            dma((7,)),
            dma((7,)),
            dma((7,)),
            dma((7,)),
            dma((n - 1,)),
            dma((n - 1,)),
        ],
        compiler_params=pltpu.CompilerParams(
            collective_id=0, has_side_effects=True, vmem_limit_bytes=44 * 2**20
        ),
        cost_estimate=pl.CostEstimate(
            flops=2 * rows * nodes * cols, bytes_accessed=8 * rows * cols, transcendentals=0
        ),
    )(owners, pattern, pruning, values)


def solution(mesh):
    nrows, ncols = mesh.shape["row"], mesh.shape["col"]

    def program(values, pattern, pruning, owners):
        rows, cols = values.shape
        packed = nrows == 8 and owners.shape[0] == 2 * ncols * ncols
        return (fused if packed else body)(values, pattern, pruning, owners)

    return jax.shard_map(
        program,
        mesh=mesh,
        in_specs=(P("row", "col"), P(), P(), P()),
        out_specs=P("row", "col"),
        check_vma=False,
    )
```

```python
import functools

import jax
import jax.numpy as jnp
from jax import lax
from jax.experimental import pallas as pl
from jax.experimental.pallas import tpu as pltpu
from jax.sharding import PartitionSpec as P

BLK = 128


def expand_mask(tile, mask, blk):
    rows_in, cols_in = tile.shape
    shaped = tile.reshape(rows_in // blk, blk, cols_in // blk, blk)
    return (shaped * mask.astype(tile.dtype)[:, None, :, None]).reshape(rows_in, cols_in)


def ranks_of(destination):
    width = destination.shape[-1]
    earlier = jnp.arange(width)[:, None] < jnp.arange(width)[None, :]
    same_dest = destination[..., :, None] == destination[..., None, :]
    return jnp.sum(jnp.where(same_dest & earlier, 1, 0), axis=-2).astype(jnp.int32)


def pack_blocks(tile, owners, me_col, ncols, capacity, blk):
    rows_in, cols_in = tile.shape
    width = cols_in // blk
    my_owners = lax.dynamic_slice(owners, (me_col * width,), (width,))
    destination = my_owners // width
    rank = ranks_of(destination)
    slot_ids = jnp.arange(ncols * capacity)
    selector = (
        (destination[None, :] == (slot_ids // capacity)[:, None])
        & (rank[None, :] == (slot_ids % capacity)[:, None])
    ).astype(tile.dtype)
    column_blocks = tile.reshape(rows_in, width, blk)
    outgoing = jnp.einsum(
        "pk,rkb->prb",
        selector,
        column_blocks,
        preferred_element_type=jnp.float32,
        precision=lax.Precision.HIGHEST,
    )
    return outgoing.astype(tile.dtype)


def unpack_blocks(arrived, owners, me_col, ncols, capacity):
    slot_count, rows_in, blk = arrived.shape
    width = owners.shape[0] // ncols
    table = owners.reshape(ncols, width)
    rank = ranks_of(table // width)
    wanted = me_col * width + jnp.arange(width)
    matches = table[None, :, :] == wanted[:, None, None]
    which_slot = rank[:, :, None] == jnp.arange(capacity)[None, None, :]
    selector = jnp.sum(jnp.where(matches[:, :, :, None] & which_slot[None], 1, 0), axis=2)
    selector = selector.reshape(width, ncols * capacity).astype(arrived.dtype)
    placed = jnp.einsum(
        "sp,prb->rsb",
        selector,
        arrived,
        preferred_element_type=jnp.float32,
        precision=lax.Precision.HIGHEST,
    )
    return placed.reshape(rows_in, width * blk).astype(arrived.dtype)


def body(values, pattern, pruning, owners):
    rows_dev, cols_dev = values.shape
    blk = BLK
    row_blocks = rows_dev // blk
    col_blocks = cols_dev // blk
    ncols = lax.axis_size("col")
    capacity = max(2, (col_blocks + ncols - 1) // ncols)
    me_row = lax.axis_index("row")
    me_col = lax.axis_index("col")
    local_pattern = lax.dynamic_slice(
        pattern, (me_row * row_blocks, me_col * col_blocks), (row_blocks, col_blocks)
    )
    masked = expand_mask(values, local_pattern, blk)
    colsum_in = lax.psum(jnp.sum(masked, axis=0), "row")
    stochastic = (masked / colsum_in[None, :]).astype(jnp.bfloat16)
    row_panel = lax.all_gather(stochastic, "col", axis=1, tiled=True)
    nodes = row_panel.shape[1]
    pruning_rows = lax.dynamic_slice(
        pruning, (me_row * row_blocks, 0), (row_blocks, pruning.shape[1])
    )
    arrived = lax.all_to_all(
        pack_blocks(stochastic, owners, me_col, ncols, capacity, blk),
        "col",
        split_axis=0,
        concat_axis=0,
        tiled=True,
    )
    right_operand = unpack_blocks(arrived, owners, me_col, ncols, capacity)
    wanted = me_col * col_blocks + jnp.arange(col_blocks)
    relocate = (owners[:, None] == wanted[None, :]).astype(jnp.float32)
    kept_mask = jnp.dot(pruning_rows.astype(jnp.float32), relocate, precision=lax.Precision.HIGHEST)
    square = jnp.dot(
        row_panel,
        lax.all_gather(right_operand, "row", axis=0, tiled=True),
        preferred_element_type=jnp.float32,
    )
    inflated = expand_mask(square * square, kept_mask, blk)
    colsum_out = lax.psum(jnp.sum(inflated, axis=0), "row")
    normalized = jnp.float32(nodes) * inflated / colsum_out[None, :]
    return normalized


MESH = pl.DeviceIdType.MESH


def kernel(n, nodes, own, pattern, pruning, values, out, tiles, right, scores, work, left, late,
           sums_a, sums_b, invs, rhs, tab, load_sem, zs, zr, xs, xr, as_, ar, bs, br, cs, cr):
    rows, cols = values.shape
    blk = BLK
    rows_b, cols_b = rows // blk, cols // blk
    nblk = n * cols_b
    wide = cols // n
    each = cols_b // n
    half = rows_b // 2
    loads = [
        pltpu.make_async_copy(values.at[:, pl.ds(b * blk, blk)], scores.at[b], load_sem.at[b])
        for b in range(cols_b)
    ]
    for load in loads:
        load.start()
    r = lax.axis_index("row")
    c = lax.axis_index("col")
    core, px, py = r % 2, (r // 2) % 2, r // 4

    def at(fy, fx, fc):
        y = 1 - py if fy else py
        x = 1 - px if fx else px
        k = 1 - core if fc else core
        return y * 4 + x * 2 + k

    others = [at(f // 4, (f // 2) % 2, f % 2) for f in range(1, 8)]

    barrier = pltpu.get_barrier_semaphore()
    for peer in others:
        pl.semaphore_signal(barrier, inc=1, device_id={"row": peer}, device_id_type=MESH)
    for d in range(1, n):
        pl.semaphore_signal(barrier, inc=1, device_id={"col": (c + d) % n}, device_id_type=MESH)

    def chosen(keys, key, options):
        found = options[0]
        for k, option in zip(keys[1:], options[1:]):
            found = jnp.where(k == key, option, found)
        return found

    def order_of(base):
        dest = [lax.div(own[base + k], cols_b) for k in range(cols_b)]
        place = []
        for k in range(cols_b):
            rank = sum([jnp.where(dest[i] == dest[k], 1, 0) for i in range(k)], 0)
            place.append(dest[k] * each + rank)
        return [chosen(place, p, range(cols_b)) for p in range(cols_b)]

    def row_copies(sums, ssem, rsem):
        return [
            pltpu.make_async_remote_copy(
                src_ref=sums.at[0], dst_ref=sums.at[f + 1], send_sem=ssem.at[f], recv_sem=rsem.at[f],
                device_id={"row": peer}, device_id_type=MESH)
            for f, peer in enumerate(others)
        ]

    def total_of(sums):
        terms = [sums[f] for f in range(8)]
        pair = [terms[i] + terms[i + 1] for i in range(0, 8, 2)]
        return (pair[0] + pair[1]) + (pair[2] + pair[3])

    def zcopy(way, d, q, source):
        target = c - 1 if way == 0 else c + 1
        return pltpu.make_async_remote_copy(
            src_ref=tiles.at[source, q], dst_ref=tiles.at[source, q],
            send_sem=zs.at[way, d, q], recv_sem=zr.at[way, d, q],
            device_id={"col": target}, device_id_type=MESH)

    def zarrive(way, d, q, source):
        peer = c + 1 if way == 0 else c - 1
        pltpu.make_async_remote_copy(
            src_ref=tiles.at[source, q], dst_ref=tiles.at[source, q],
            send_sem=zs.at[way, d, q], recv_sem=zr.at[way, d, q],
            device_id={"col": peer}, device_id_type=MESH).wait_recv()

    side_x, side_y, side_c = at(0, 1, 0), at(1, 0, 0), at(0, 0, 1)
    diag = at(1, 1, 0)

    def region(u, who, part):
        if part is None:
            return right.at[u, pl.ds(who * rows_b, rows_b)]
        return right.at[u, pl.ds(who * rows_b + part * half, half)]

    def sent(u, k):
        src, dst, to = [
            (region(u, r, None), region(u, r, None), side_x),
            (region(u, r, None), region(u, r, None), side_y),
            (region(u, r, None), region(u, r, None), side_c),
            (region(u, side_x, 0), region(u, side_x, 0), side_y),
            (region(u, side_y, 1), region(u, side_y, 1), side_x),
            (region(u, side_x, None), region(u, side_x, None), side_c),
            (region(u, side_y, None), region(u, side_y, None), side_c),
            (region(u, diag, 0), region(u, diag, 0), side_c),
            (region(u, diag, 1), region(u, diag, 1), side_c),
        ][k]
        return pltpu.make_async_remote_copy(
            src_ref=src, dst_ref=dst, send_sem=xs.at[u, k], recv_sem=xr.at[u, k],
            device_id={"row": to}, device_id_type=MESH)

    def landed(u, k):
        where, to = [
            (region(u, side_x, None), side_x),
            (region(u, side_y, None), side_y),
            (region(u, side_c, None), side_c),
            (region(u, diag, 0), side_y),
            (region(u, diag, 1), side_x),
            (region(u, at(0, 1, 1), None), side_c),
            (region(u, at(1, 0, 1), None), side_c),
            (region(u, at(1, 1, 1), 0), side_c),
            (region(u, at(1, 1, 1), 1), side_c),
        ][k]
        pltpu.make_async_remote_copy(
            src_ref=where, dst_ref=where, send_sem=xs.at[u, k], recv_sem=xr.at[u, k],
            device_id={"row": to}, device_id_type=MESH).wait_recv()

    def begin(u):
        right[u, pl.ds(r * rows_b, rows_b)] = tiles[u, c].reshape(rows_b, blk, wide)
        for k in range(3):
            sent(u, k).start()

    def second(u):
        landed(u, 0)
        sent(u, 3).start()
        sent(u, 5).start()
        landed(u, 1)
        sent(u, 4).start()
        sent(u, 6).start()

    def third(u):
        landed(u, 3)
        sent(u, 7).start()
        landed(u, 4)
        sent(u, 8).start()

    mine = order_of(c * cols_b)
    for load in loads:
        load.wait()
    pl.semaphore_wait(barrier, 7 + n - 1)
    made = []
    for i in range((n + 1) // 2):
        made += [i, n - 1 - i] if i != n - 1 - i else [i]
    for q in made:
        for k in range(each):
            b = mine[q * each + k]
            acc = jnp.zeros((1, blk), jnp.float32)
            for i in range(rows_b):
                keep = pattern[r * rows_b + i, c * cols_b + b].astype(jnp.float32)
                x = scores[b, pl.ds(i * blk, blk), :] * keep
                tiles[c, q, pl.ds(i * blk, blk), pl.ds(k * blk, blk)] = x.astype(jnp.bfloat16)
                acc = acc + jnp.sum(x, axis=0, keepdims=True)
            sums_a[0, q, :, pl.ds(k * blk, blk)] = acc

        @pl.when(c > 0)
        def _():
            zcopy(0, 0, q, c).start()

        @pl.when(c < n - 1)
        def _():
            zcopy(1, 0, q, c).start()
    for copy in row_copies(sums_a, as_, ar):
        copy.start()
    begin(c)

    for z in range(n):
        for p, b in enumerate(order_of(z * cols_b)):
            tab[z * cols_b + p] = z * cols_b + b
    came = [tab[u * cols_b + c * each + k] for u in range(n) for k in range(each)]
    goes = [own[b] - c * cols_b for b in came]

    for copy in row_copies(sums_a, as_, ar):
        copy.wait()
    invs[c] = 1.0 / total_of(sums_a)

    def scales(d):
        return pltpu.make_async_remote_copy(
            src_ref=invs.at[c], dst_ref=invs.at[c], send_sem=cs.at[d - 1], recv_sem=cr.at[d - 1],
            device_id={"col": (c + d) % n}, device_id_type=MESH)

    for d in range(1, n):
        scales(d).start()

    def scales_landed():
        for d in range(1, n):
            source = (c + n - d) % n
            pltpu.make_async_remote_copy(
                src_ref=invs.at[source], dst_ref=invs.at[source],
                send_sem=cs.at[d - 1], recv_sem=cr.at[d - 1],
                device_id={"col": source}, device_id_type=MESH).wait_recv()

    last = jnp.where(c < n // 2, n - 1, 0)

    def scaled(z, q):
        return (tiles[z, q].astype(jnp.float32) * invs[z, q]).astype(jnp.bfloat16)

    def early_product():
        scales_landed()
        for u in range(n):
            for k in (2, 5, 6, 7, 8):
                landed(u, k)
        for z in range(n):
            for j in range(n - 1):
                left[:, pl.ds(j * wide, wide)] = scaled(z, (last + 1 + j) % n)

            def product(u, carry):
                for j in range(n - 1):
                    q = (last + 1 + j) % n
                    for k in range(each):
                        rhs[pl.ds((j * each + k) * blk, blk), :] = right[u, tab[z * cols_b + q * each + k]]
                part = jnp.dot(
                    left[...], rhs[pl.ds(0, (n - 1) * wide), :], preferred_element_type=jnp.float32)
                for k in range(each):
                    cut = part[:, k * blk:(k + 1) * blk]
                    if z == 0:
                        work[u * each + k] = cut
                    else:
                        work[u * each + k] += cut
                return carry
            lax.fori_loop(0, n, product, 0)

    def late_product():
        for z in range(n):
            late[:, pl.ds(z * wide, wide)] = scaled(z, last)

        def product(u, carry):
            for z in range(n):
                for k in range(each):
                    rhs[pl.ds((z * each + k) * blk, blk), :] = right[u, tab[z * cols_b + last * each + k]]
            part = jnp.dot(late[...], rhs[...], preferred_element_type=jnp.float32)
            scale = invs[u, c]
            for k in range(each):
                piece = slice(k * blk, (k + 1) * blk)
                work[u * each + k] = (work[u * each + k] + part[:, piece]) * scale[:, piece]
            return carry
        lax.fori_loop(0, n, product, 0)

    at_end = (c == 0) | (c == n - 1)

    def begun_at(stage, act):
        if stage == -1:
            act(c)
        for d in range(1, n):
            @pl.when((c == stage) & (c + d < n))
            def _():
                act(c + d)

            @pl.when((n - 1 - c == stage) & (c - d >= 0))
            def _():
                act(c - d)

    for i in range(n + 1):
        if i == n - 1:
            @pl.when(at_end)
            def _():
                early_product()
        if i < n:
            for d in range(1, n):
                @pl.when(c + d < n)
                def _():
                    zarrive(0, d - 1, i, c + d)

                    @pl.when(c > 0)
                    def _():
                        if d < n - 1:
                            zcopy(0, d, i, c + d).start()

                    @pl.when(c == i)
                    def _():
                        begin(c + d)

                @pl.when(c - d >= 0)
                def _():
                    zarrive(1, d - 1, n - 1 - i, c - d)

                    @pl.when(c < n - 1)
                    def _():
                        if d < n - 1:
                            zcopy(1, d, n - 1 - i, c - d).start()

                    @pl.when(c == n - 1 - i)
                    def _():
                        begin(c - d)
        begun_at(i - 1, second)
        begun_at(i - 2, third)
    begun_at(n - 1, third)

    @pl.when(jnp.logical_not(at_end))
    def _():
        early_product()

    late_product()

    for s in range(cols_b):
        p = chosen(goes, s, range(cols_b))
        b = chosen(goes, s, came)
        acc = jnp.zeros((1, blk), jnp.float32)
        for i in range(rows_b):
            keep = pruning[r * rows_b + i, b].astype(jnp.float32)
            x = work[p, pl.ds(i * blk, blk), :]
            x = x * x * keep
            out[pl.ds(i * blk, blk), pl.ds(s * blk, blk)] = x
            acc = acc + jnp.sum(x, axis=0, keepdims=True)
        sums_b[0, :, pl.ds(s * blk, blk)] = acc
    for copy in row_copies(sums_b, bs, br):
        copy.start()
    for copy in row_copies(sums_b, bs, br):
        copy.wait()
    inv_out = 1.0 / total_of(sums_b)
    out[...] = (out[...] * inv_out) * jnp.float32(nodes)

    for d in range(1, n):
        scales(d).wait_send()
    for i in range(n):
        for d in range(n - 1):
            @pl.when((c > 0) & (c + d < n))
            def _():
                zcopy(0, d, i, c + d).wait_send()

            @pl.when((c < n - 1) & (c - d >= 0))
            def _():
                zcopy(1, d, i, c - d).wait_send()
    for u in range(n):
        for k in range(9):
            sent(u, k).wait_send()


def fused(values, pattern, pruning, owners):
    rows, cols = values.shape
    n = lax.axis_size("col")
    nodes = n * cols
    dma = pltpu.SemaphoreType.DMA
    return pl.pallas_call(
        functools.partial(kernel, n, nodes),
        out_shape=jax.ShapeDtypeStruct((rows, cols), jnp.float32),
        in_specs=[pl.BlockSpec(memory_space=pltpu.SMEM)] * 3 + [pl.BlockSpec(memory_space=pl.ANY)],
        out_specs=pl.BlockSpec(memory_space=pltpu.VMEM),
        scratch_shapes=[
            pltpu.VMEM((n, n, rows, cols // n), jnp.bfloat16),
            pltpu.VMEM((n, nodes // BLK, BLK, cols // n), jnp.bfloat16),
            pltpu.VMEM((cols // BLK, rows, BLK), jnp.float32),
            pltpu.VMEM((cols // BLK, rows, BLK), jnp.float32),
            pltpu.VMEM((rows, cols - cols // n), jnp.bfloat16),
            pltpu.VMEM((rows, cols), jnp.bfloat16),
            pltpu.VMEM((8, n, 1, cols // n), jnp.float32),
            pltpu.VMEM((8, 1, cols), jnp.float32),
            pltpu.VMEM((n, n, 1, cols // n), jnp.float32),
            pltpu.VMEM((cols, cols // n), jnp.bfloat16),
            pltpu.SMEM((nodes // BLK,), jnp.int32),
            dma((cols // BLK,)),
            dma((2, n - 1, n)),
            dma((2, n - 1, n)),
            dma((n, 9)),
            dma((n, 9)),
            dma((7,)),
            dma((7,)),
            dma((7,)),
            dma((7,)),
            dma((n - 1,)),
            dma((n - 1,)),
        ],
        compiler_params=pltpu.CompilerParams(
            collective_id=0, has_side_effects=True, vmem_limit_bytes=62 * 2**20
        ),
        cost_estimate=pl.CostEstimate(
            flops=2 * rows * nodes * cols, bytes_accessed=8 * rows * cols, transcendentals=0
        ),
    )(owners, pattern, pruning, values)


def solution(mesh):
    nrows, ncols = mesh.shape["row"], mesh.shape["col"]

    def program(values, pattern, pruning, owners):
        rows, cols = values.shape
        packed = nrows == 8 and owners.shape[0] == 2 * ncols * ncols
        return (fused if packed else body)(values, pattern, pruning, owners)

    return jax.shard_map(
        program,
        mesh=mesh,
        in_specs=(P("row", "col"), P(), P(), P()),
        out_specs=P("row", "col"),
        check_vma=False,
    )
```

```python
import functools

import jax
import jax.numpy as jnp
from jax import lax
from jax.experimental import pallas as pl
from jax.experimental.pallas import tpu as pltpu
from jax.sharding import PartitionSpec as P

BLK = 128


def expand_mask(tile, mask, blk):
    rows_in, cols_in = tile.shape
    shaped = tile.reshape(rows_in // blk, blk, cols_in // blk, blk)
    return (shaped * mask.astype(tile.dtype)[:, None, :, None]).reshape(rows_in, cols_in)


def ranks_of(destination):
    width = destination.shape[-1]
    earlier = jnp.arange(width)[:, None] < jnp.arange(width)[None, :]
    same_dest = destination[..., :, None] == destination[..., None, :]
    return jnp.sum(jnp.where(same_dest & earlier, 1, 0), axis=-2).astype(jnp.int32)


def pack_blocks(tile, owners, me_col, ncols, capacity, blk):
    rows_in, cols_in = tile.shape
    width = cols_in // blk
    my_owners = lax.dynamic_slice(owners, (me_col * width,), (width,))
    destination = my_owners // width
    rank = ranks_of(destination)
    slot_ids = jnp.arange(ncols * capacity)
    selector = (
        (destination[None, :] == (slot_ids // capacity)[:, None])
        & (rank[None, :] == (slot_ids % capacity)[:, None])
    ).astype(tile.dtype)
    column_blocks = tile.reshape(rows_in, width, blk)
    outgoing = jnp.einsum(
        "pk,rkb->prb",
        selector,
        column_blocks,
        preferred_element_type=jnp.float32,
        precision=lax.Precision.HIGHEST,
    )
    return outgoing.astype(tile.dtype)


def unpack_blocks(arrived, owners, me_col, ncols, capacity):
    slot_count, rows_in, blk = arrived.shape
    width = owners.shape[0] // ncols
    table = owners.reshape(ncols, width)
    rank = ranks_of(table // width)
    wanted = me_col * width + jnp.arange(width)
    matches = table[None, :, :] == wanted[:, None, None]
    which_slot = rank[:, :, None] == jnp.arange(capacity)[None, None, :]
    selector = jnp.sum(jnp.where(matches[:, :, :, None] & which_slot[None], 1, 0), axis=2)
    selector = selector.reshape(width, ncols * capacity).astype(arrived.dtype)
    placed = jnp.einsum(
        "sp,prb->rsb",
        selector,
        arrived,
        preferred_element_type=jnp.float32,
        precision=lax.Precision.HIGHEST,
    )
    return placed.reshape(rows_in, width * blk).astype(arrived.dtype)


def body(values, pattern, pruning, owners):
    rows_dev, cols_dev = values.shape
    blk = BLK
    row_blocks = rows_dev // blk
    col_blocks = cols_dev // blk
    ncols = lax.axis_size("col")
    capacity = max(2, (col_blocks + ncols - 1) // ncols)
    me_row = lax.axis_index("row")
    me_col = lax.axis_index("col")
    local_pattern = lax.dynamic_slice(
        pattern, (me_row * row_blocks, me_col * col_blocks), (row_blocks, col_blocks)
    )
    masked = expand_mask(values, local_pattern, blk)
    colsum_in = lax.psum(jnp.sum(masked, axis=0), "row")
    stochastic = (masked / colsum_in[None, :]).astype(jnp.bfloat16)
    row_panel = lax.all_gather(stochastic, "col", axis=1, tiled=True)
    nodes = row_panel.shape[1]
    pruning_rows = lax.dynamic_slice(
        pruning, (me_row * row_blocks, 0), (row_blocks, pruning.shape[1])
    )
    arrived = lax.all_to_all(
        pack_blocks(stochastic, owners, me_col, ncols, capacity, blk),
        "col",
        split_axis=0,
        concat_axis=0,
        tiled=True,
    )
    right_operand = unpack_blocks(arrived, owners, me_col, ncols, capacity)
    wanted = me_col * col_blocks + jnp.arange(col_blocks)
    relocate = (owners[:, None] == wanted[None, :]).astype(jnp.float32)
    kept_mask = jnp.dot(pruning_rows.astype(jnp.float32), relocate, precision=lax.Precision.HIGHEST)
    square = jnp.dot(
        row_panel,
        lax.all_gather(right_operand, "row", axis=0, tiled=True),
        preferred_element_type=jnp.float32,
    )
    inflated = expand_mask(square * square, kept_mask, blk)
    colsum_out = lax.psum(jnp.sum(inflated, axis=0), "row")
    normalized = jnp.float32(nodes) * inflated / colsum_out[None, :]
    return normalized


MESH = pl.DeviceIdType.MESH


def kernel(n, nodes, own, pattern, pruning, values, out, tiles, right, scores, work, left, late,
           sums_a, sums_b, invs, rhs, tab, load_sem, zs, zr, xs, xr, as_, ar, bs, br, cs, cr):
    rows, cols = values.shape
    blk = BLK
    rows_b, cols_b = rows // blk, cols // blk
    nblk = n * cols_b
    wide = cols // n
    each = cols_b // n
    half = rows_b // 2
    loads = [
        pltpu.make_async_copy(values.at[:, pl.ds(b * blk, blk)], scores.at[b], load_sem.at[b])
        for b in range(cols_b)
    ]
    for load in loads:
        load.start()
    r = lax.axis_index("row")
    c = lax.axis_index("col")
    core, px, py = r % 2, (r // 2) % 2, r // 4

    def at(fy, fx, fc):
        y = 1 - py if fy else py
        x = 1 - px if fx else px
        k = 1 - core if fc else core
        return y * 4 + x * 2 + k

    others = [at(f // 4, (f // 2) % 2, f % 2) for f in range(1, 8)]

    barrier = pltpu.get_barrier_semaphore()
    for peer in others:
        pl.semaphore_signal(barrier, inc=1, device_id={"row": peer}, device_id_type=MESH)
    for d in range(1, n):
        pl.semaphore_signal(barrier, inc=1, device_id={"col": (c + d) % n}, device_id_type=MESH)

    def chosen(keys, key, options):
        found = options[0]
        for k, option in zip(keys[1:], options[1:]):
            found = jnp.where(k == key, option, found)
        return found

    def order_of(base):
        dest = [lax.div(own[base + k], cols_b) for k in range(cols_b)]
        place = []
        for k in range(cols_b):
            rank = sum([jnp.where(dest[i] == dest[k], 1, 0) for i in range(k)], 0)
            place.append(dest[k] * each + rank)
        return [chosen(place, p, range(cols_b)) for p in range(cols_b)]

    def row_copies(sums, ssem, rsem):
        return [
            pltpu.make_async_remote_copy(
                src_ref=sums.at[0], dst_ref=sums.at[f + 1], send_sem=ssem.at[f], recv_sem=rsem.at[f],
                device_id={"row": peer}, device_id_type=MESH)
            for f, peer in enumerate(others)
        ]

    def total_of(sums):
        terms = [sums[f] for f in range(8)]
        pair = [terms[i] + terms[i + 1] for i in range(0, 8, 2)]
        return (pair[0] + pair[1]) + (pair[2] + pair[3])

    def zcopy(way, d, q, source):
        target = c - 1 if way == 0 else c + 1
        return pltpu.make_async_remote_copy(
            src_ref=tiles.at[source, q], dst_ref=tiles.at[source, q],
            send_sem=zs.at[way, d, q], recv_sem=zr.at[way, d, q],
            device_id={"col": target}, device_id_type=MESH)

    def zarrive(way, d, q, source):
        peer = c + 1 if way == 0 else c - 1
        pltpu.make_async_remote_copy(
            src_ref=tiles.at[source, q], dst_ref=tiles.at[source, q],
            send_sem=zs.at[way, d, q], recv_sem=zr.at[way, d, q],
            device_id={"col": peer}, device_id_type=MESH).wait_recv()

    side_x, side_y, side_c = at(0, 1, 0), at(1, 0, 0), at(0, 0, 1)
    diag = at(1, 1, 0)

    def region(u, who, part):
        if part is None:
            return right.at[u, pl.ds(who * rows_b, rows_b)]
        return right.at[u, pl.ds(who * rows_b + part * half, half)]

    def sent(u, k):
        src, dst, to = [
            (region(u, r, None), region(u, r, None), side_x),
            (region(u, r, None), region(u, r, None), side_y),
            (region(u, r, None), region(u, r, None), side_c),
            (region(u, side_x, 0), region(u, side_x, 0), side_y),
            (region(u, side_y, 1), region(u, side_y, 1), side_x),
            (region(u, side_x, None), region(u, side_x, None), side_c),
            (region(u, side_y, None), region(u, side_y, None), side_c),
            (region(u, diag, 0), region(u, diag, 0), side_c),
            (region(u, diag, 1), region(u, diag, 1), side_c),
        ][k]
        return pltpu.make_async_remote_copy(
            src_ref=src, dst_ref=dst, send_sem=xs.at[u, k], recv_sem=xr.at[u, k],
            device_id={"row": to}, device_id_type=MESH)

    def landed(u, k):
        where, to = [
            (region(u, side_x, None), side_x),
            (region(u, side_y, None), side_y),
            (region(u, side_c, None), side_c),
            (region(u, diag, 0), side_y),
            (region(u, diag, 1), side_x),
            (region(u, at(0, 1, 1), None), side_c),
            (region(u, at(1, 0, 1), None), side_c),
            (region(u, at(1, 1, 1), 0), side_c),
            (region(u, at(1, 1, 1), 1), side_c),
        ][k]
        pltpu.make_async_remote_copy(
            src_ref=where, dst_ref=where, send_sem=xs.at[u, k], recv_sem=xr.at[u, k],
            device_id={"row": to}, device_id_type=MESH).wait_recv()

    def begin(u):
        right[u, pl.ds(r * rows_b, rows_b)] = tiles[u, c].reshape(rows_b, blk, wide)
        for k in range(3):
            sent(u, k).start()

    def second(u):
        landed(u, 0)
        sent(u, 3).start()
        sent(u, 5).start()
        landed(u, 1)
        sent(u, 4).start()
        sent(u, 6).start()

    def third(u):
        landed(u, 3)
        sent(u, 7).start()
        landed(u, 4)
        sent(u, 8).start()

    mine = order_of(c * cols_b)
    for load in loads:
        load.wait()
    pl.semaphore_wait(barrier, 7 + n - 1)
    made = []
    for i in range((n + 1) // 2):
        made += [i, n - 1 - i] if i != n - 1 - i else [i]
    for q in made:
        for k in range(each):
            b = mine[q * each + k]
            acc = jnp.zeros((1, blk), jnp.float32)
            for i in range(rows_b):
                keep = pattern[r * rows_b + i, c * cols_b + b].astype(jnp.float32)
                x = scores[b, pl.ds(i * blk, blk), :] * keep
                tiles[c, q, pl.ds(i * blk, blk), pl.ds(k * blk, blk)] = x.astype(jnp.bfloat16)
                acc = acc + jnp.sum(x, axis=0, keepdims=True)
            sums_a[0, q, :, pl.ds(k * blk, blk)] = acc

        @pl.when(c > 0)
        def _():
            zcopy(0, 0, q, c).start()

        @pl.when(c < n - 1)
        def _():
            zcopy(1, 0, q, c).start()
    for copy in row_copies(sums_a, as_, ar):
        copy.start()
    begin(c)

    for z in range(n):
        for p, b in enumerate(order_of(z * cols_b)):
            tab[z * cols_b + p] = z * cols_b + b
    came = [tab[u * cols_b + c * each + k] for u in range(n) for k in range(each)]
    goes = [own[b] - c * cols_b for b in came]

    for copy in row_copies(sums_a, as_, ar):
        copy.wait()
    invs[c] = 1.0 / total_of(sums_a)

    def scales(d):
        return pltpu.make_async_remote_copy(
            src_ref=invs.at[c], dst_ref=invs.at[c], send_sem=cs.at[d - 1], recv_sem=cr.at[d - 1],
            device_id={"col": (c + d) % n}, device_id_type=MESH)

    for d in range(1, n):
        scales(d).start()

    def scales_landed():
        for d in range(1, n):
            source = (c + n - d) % n
            pltpu.make_async_remote_copy(
                src_ref=invs.at[source], dst_ref=invs.at[source],
                send_sem=cs.at[d - 1], recv_sem=cr.at[d - 1],
                device_id={"col": source}, device_id_type=MESH).wait_recv()

    last = jnp.where(c < n // 2, n - 1, 0)

    def scaled(z, q):
        return (tiles[z, q].astype(jnp.float32) * invs[z, q]).astype(jnp.bfloat16)

    def early_product():
        scales_landed()
        for u in range(n):
            for k in (2, 5, 6, 7, 8):
                landed(u, k)
        for z in range(n):
            for j in range(n - 1):
                left[:, pl.ds(j * wide, wide)] = scaled(z, (last + 1 + j) % n)

            def product(u, carry):
                for j in range(n - 1):
                    q = (last + 1 + j) % n
                    for k in range(each):
                        rhs[pl.ds((j * each + k) * blk, blk), :] = right[u, tab[z * cols_b + q * each + k]]
                part = jnp.dot(
                    left[...], rhs[pl.ds(0, (n - 1) * wide), :], preferred_element_type=jnp.float32)
                for k in range(each):
                    cut = part[:, k * blk:(k + 1) * blk]
                    if z == 0:
                        work[u * each + k] = cut
                    else:
                        work[u * each + k] += cut
                return carry
            lax.fori_loop(0, n, product, 0)

    def late_product():
        for z in range(n):
            late[:, pl.ds(z * wide, wide)] = scaled(z, last)

        def product(u, carry):
            for z in range(n):
                for k in range(each):
                    rhs[pl.ds((z * each + k) * blk, blk), :] = right[u, tab[z * cols_b + last * each + k]]
            part = jnp.dot(late[...], rhs[...], preferred_element_type=jnp.float32)
            scale = invs[u, c]
            for k in range(each):
                piece = slice(k * blk, (k + 1) * blk)
                work[u * each + k] = (work[u * each + k] + part[:, piece]) * scale[:, piece]
            return carry
        lax.fori_loop(0, n, product, 0)

    at_end = (c == 0) | (c == n - 1)

    def begun_at(stage, act):
        if stage == -1:
            act(c)
        for d in range(1, n):
            @pl.when((c == stage) & (c + d < n))
            def _():
                act(c + d)

            @pl.when((n - 1 - c == stage) & (c - d >= 0))
            def _():
                act(c - d)

    for i in range(n + 1):
        if i == n - 1:
            @pl.when(at_end)
            def _():
                early_product()
        if i < n:
            for d in range(1, n):
                @pl.when(c + d < n)
                def _():
                    zarrive(0, d - 1, i, c + d)

                    @pl.when(c > 0)
                    def _():
                        if d < n - 1:
                            zcopy(0, d, i, c + d).start()

                    @pl.when(c == i)
                    def _():
                        begin(c + d)

                @pl.when(c - d >= 0)
                def _():
                    zarrive(1, d - 1, n - 1 - i, c - d)

                    @pl.when(c < n - 1)
                    def _():
                        if d < n - 1:
                            zcopy(1, d, n - 1 - i, c - d).start()

                    @pl.when(c == n - 1 - i)
                    def _():
                        begin(c - d)
        begun_at(i - 1, second)
        begun_at(i - 2, third)
    begun_at(n - 1, third)

    @pl.when(jnp.logical_not(at_end))
    def _():
        early_product()

    late_product()

    for s in range(cols_b):
        p = chosen(goes, s, range(cols_b))
        b = chosen(goes, s, came)
        acc = jnp.zeros((1, blk), jnp.float32)
        for i in range(rows_b):
            keep = pruning[r * rows_b + i, b].astype(jnp.float32)
            x = work[p, pl.ds(i * blk, blk), :]
            x = x * x * keep
            out[pl.ds(i * blk, blk), pl.ds(s * blk, blk)] = x
            acc = acc + jnp.sum(x, axis=0, keepdims=True)
        sums_b[0, :, pl.ds(s * blk, blk)] = acc
    for copy in row_copies(sums_b, bs, br):
        copy.start()
    for copy in row_copies(sums_b, bs, br):
        copy.wait()
    inv_out = 1.0 / total_of(sums_b)
    out[...] = out[...] * inv_out

    for d in range(1, n):
        scales(d).wait_send()
    for i in range(n):
        for d in range(n - 1):
            @pl.when((c > 0) & (c + d < n))
            def _():
                zcopy(0, d, i, c + d).wait_send()

            @pl.when((c < n - 1) & (c - d >= 0))
            def _():
                zcopy(1, d, i, c - d).wait_send()
    for u in range(n):
        for k in range(9):
            sent(u, k).wait_send()


def fused(values, pattern, pruning, owners):
    rows, cols = values.shape
    n = lax.axis_size("col")
    nodes = n * cols
    dma = pltpu.SemaphoreType.DMA
    shares = pl.pallas_call(
        functools.partial(kernel, n, nodes),
        out_shape=jax.ShapeDtypeStruct((rows, cols), jnp.float32),
        in_specs=[pl.BlockSpec(memory_space=pltpu.SMEM)] * 3 + [pl.BlockSpec(memory_space=pl.ANY)],
        out_specs=pl.BlockSpec(memory_space=pltpu.VMEM),
        scratch_shapes=[
            pltpu.VMEM((n, n, rows, cols // n), jnp.bfloat16),
            pltpu.VMEM((n, nodes // BLK, BLK, cols // n), jnp.bfloat16),
            pltpu.VMEM((cols // BLK, rows, BLK), jnp.float32),
            pltpu.VMEM((cols // BLK, rows, BLK), jnp.float32),
            pltpu.VMEM((rows, cols - cols // n), jnp.bfloat16),
            pltpu.VMEM((rows, cols), jnp.bfloat16),
            pltpu.VMEM((8, n, 1, cols // n), jnp.float32),
            pltpu.VMEM((8, 1, cols), jnp.float32),
            pltpu.VMEM((n, n, 1, cols // n), jnp.float32),
            pltpu.VMEM((cols, cols // n), jnp.bfloat16),
            pltpu.SMEM((nodes // BLK,), jnp.int32),
            dma((cols // BLK,)),
            dma((2, n - 1, n)),
            dma((2, n - 1, n)),
            dma((n, 9)),
            dma((n, 9)),
            dma((7,)),
            dma((7,)),
            dma((7,)),
            dma((7,)),
            dma((n - 1,)),
            dma((n - 1,)),
        ],
        compiler_params=pltpu.CompilerParams(
            collective_id=0, has_side_effects=True, vmem_limit_bytes=62 * 2**20
        ),
        cost_estimate=pl.CostEstimate(
            flops=2 * rows * nodes * cols, bytes_accessed=8 * rows * cols, transcendentals=0
        ),
    )(owners, pattern, pruning, values)
    return jnp.float32(nodes) * shares


def solution(mesh):
    nrows, ncols = mesh.shape["row"], mesh.shape["col"]

    def program(values, pattern, pruning, owners):
        rows, cols = values.shape
        packed = nrows == 8 and owners.shape[0] == 2 * ncols * ncols
        return (fused if packed else body)(values, pattern, pruning, owners)

    return jax.shard_map(
        program,
        mesh=mesh,
        in_specs=(P("row", "col"), P(), P(), P()),
        out_specs=P("row", "col"),
        check_vma=False,
    )
```
